32 devices in a mesh: runs: 2 (over x), tm: 8 (over z, y), hyd: 2 (over core).
Axes of the slice: x: 2, y: 2, z: 4, core: 2. Of those that a mesh axis runs over, the one named last changes fastest.
Arguments:
- record: bfloat16 [524160, 1024], P(('runs', 'tm'), 'hyd'), parts along dimension 0, may hold values from -6 to 6
- chips: int32 [4095], replicated, may hold values from -1 to 1, as said below
- steer_lags: int32 [1024, 256], P('hyd'), may hold values from 0 to 7
Outputs:
- power: float32 [128, 512, 256], P('runs', 'tm', 'hyd'), parts along dimension 0
The draws below stay inside these ranges and needn't reach their ends.
There are 2 independent parts, one for each index of `runs`. The reference program is written for one: setup_inputs(seed, part) draws one part's arguments, and reference() takes and returns one part's arrays. A program takes and returns all parts, laid end to end along the dimension named above; an argument that names none is the same for every part. Nothing has to cross between parts.
Inputs may be any that keep to these rules, and one draw needn't show every extreme that they name: The chips are +1 or -1 and form one period of a maximal-length sequence of period 4095, starting at a drawn phase.
All inputs are finite; a program needn't handle non-finite values.
Results may differ from the reference program's by a relative error of at most 0.0047.
Values may be sent and summed in bfloat16 or wider, within the bound.
A program may use at most 256 MiB of HBM per device.

```python
import math
import jax
import jax.numpy as jnp
from jax import lax

CODE = 4095
HYDRO = 1024
DELAYS = 512
PERIODS = 64
BEAMS = 256
MAXLAG = 8
SAMPLES = 262080


feedback_taps = {5: (0, 2), 6: (0, 1), 7: (0, 1), 8: (0, 2, 3, 4), 9: (0, 4), 10: (0, 3), 11: (0, 2), 12: (0, 1, 4, 6)}


def draw_chips(key, part):
    degree = (CODE + 1).bit_length() - 1
    feedback = feedback_taps[degree]
    seed_state = jax.random.randint(key, (), 1, 2 ** degree, dtype=jnp.int32)
    register = jnp.right_shift(seed_state, jnp.arange(degree, dtype=jnp.int32)) & 1

    def advance(register, unused):
        incoming = reduce_bits(register, feedback)
        return (jnp.concatenate([register[1:], incoming[None]]), register[0])
    final_state, chip_bits = lax.scan(advance, register, None, length=CODE)
    return (1 - 2 * chip_bits).astype(jnp.int32)


def reduce_bits(register, feedback):
    summed = register[feedback[0]]
    for position in feedback[1:]:
        summed = summed + register[position]
    return summed % 2


def plant(entries, key, smallest, top_value):
    longest = entries.shape.index(max(entries.shape))
    spots = []
    for shift in (0, 1):
        where = [jax.random.randint(jax.random.fold_in(key, axis), (), 0, length) for axis, length in enumerate(entries.shape)]
        where[longest] = (where[longest] + shift) % entries.shape[longest]
        spots.append(tuple(where))
    return entries.at[spots[0]].set(smallest).at[spots[1]].set(top_value)


def level_of(own_key, shape, shards, low, largest):
    gain = 1.0
    for axis_at, shards_of in shards:
        draws = jax.random.uniform(jax.random.fold_in(jax.random.fold_in(own_key, 6), axis_at), (shards_of,), jnp.float32, low / len(shards), largest / len(shards))
        gain = gain * jnp.repeat(jnp.exp(draws), shape[axis_at] // shards_of).reshape((-1,) + (1,) * (len(shape) - 1 - axis_at))
    return gain


def noise(stream_key, extent, spread, reach, cuts=(), kind=jnp.bfloat16):
    factor_of = level_of(stream_key, extent, cuts, -0.22, 0.18) if cuts else 1.0
    array = jax.random.normal(stream_key, extent, jnp.float32) * spread * factor_of
    return jnp.minimum(jnp.maximum(array, -reach), reach).astype(kind)


def setup_inputs(seed: int = 0, part: int = 0) -> dict:
    splits = jax.random.split(jax.random.key(seed), 4)
    part_keys = jax.random.split(jax.random.fold_in(splits[3], part), 4)
    record = noise(part_keys[0], (SAMPLES, HYDRO), 1.0, 6.0, ((0, 8), (1, 2)))
    chips = draw_chips(jax.random.fold_in(splits[3], 71), part)
    steer_lags = plant(jax.random.randint(splits[2], (HYDRO, BEAMS), 0, MAXLAG), jax.random.fold_in(splits[2], 1), 0, MAXLAG - 1).astype(jnp.int32)
    return dict(record=record, chips=chips, steer_lags=steer_lags)


def toeplitz_code(chips):
    seg_len = CODE + DELAYS - 1
    padded = jnp.concatenate([chips.astype(jnp.float32), jnp.zeros((DELAYS,), jnp.float32)])
    tiled = jnp.tile(padded, DELAYS)[:DELAYS * seg_len]
    return tiled.reshape(DELAYS, seg_len).astype(jnp.bfloat16)

def dft_table(length):
    freq = jnp.arange(length, dtype=jnp.int32)
    phase = (freq[:, None] * freq[None, :] % length).astype(jnp.float32) * (2.0 * math.pi / length)
    weight = 1.0 / math.sqrt(length)
    return jnp.concatenate([jnp.cos(phase) * weight, -jnp.sin(phase) * weight], 0).astype(jnp.bfloat16)

def reference(record, chips, steer_lags):
    seg_len = CODE + DELAYS - 1
    toeplitz = toeplitz_code(chips)
    padded = jnp.concatenate([record, jnp.zeros((DELAYS - 1, HYDRO), jnp.bfloat16)], 0)
    norm_code = 1.0 / math.sqrt(CODE)

    def correlate(period):
        segment = lax.dynamic_slice_in_dim(padded, period * CODE, seg_len, 0)
        return (jnp.dot(toeplitz, segment, preferred_element_type=jnp.float32) * norm_code).astype(jnp.bfloat16)
    profiles = lax.map(correlate, jnp.arange(PERIODS, dtype=jnp.int32))
    spectrum = jnp.dot(dft_table(PERIODS), profiles.reshape(PERIODS, DELAYS * HYDRO), preferred_element_type=jnp.float32)
    spectrum = spectrum.astype(jnp.bfloat16).reshape(2, PERIODS, DELAYS, HYDRO)
    widened = jnp.concatenate([spectrum, jnp.zeros((2, PERIODS, MAXLAG - 1, HYDRO), jnp.bfloat16)], 2)
    partial_sum = jnp.zeros((2 * PERIODS * DELAYS, BEAMS), jnp.float32)
    for offset in range(MAXLAG):
        selector = (steer_lags == offset).astype(jnp.bfloat16)
        shifted = widened[:, :, offset:offset + DELAYS, :].reshape(2 * PERIODS * DELAYS, HYDRO)
        partial_sum = partial_sum + jnp.dot(shifted, selector, preferred_element_type=jnp.float32)
    beam = (partial_sum * (1.0 / math.sqrt(HYDRO))).reshape(2, PERIODS, DELAYS, BEAMS)
    return beam[0] * beam[0] + beam[1] * beam[1]
```

```python
import functools
import math

import jax
import jax.numpy as jnp
from jax import lax
from jax.experimental import pallas as pl
from jax.experimental.pallas import tpu as pltpu
from jax.sharding import PartitionSpec as P

CODE = 4095
HYDRO = 1024
DELAYS = 512
PERIODS = 64
BEAMS = 256
MAXLAG = 8

ROWS = 8
STEP = DELAYS // ROWS
OUT_ROWS = ROWS * (STEP + MAXLAG)
CODE_ROWS = OUT_ROWS + ROWS * 14
WIDTH = 4736
MAIN = 4096
EXTRA = WIDTH - MAIN
LATE = 528
MESH = pl.DeviceIdType.MESH


def build_code(base_ref, code_ref):
    def fill(pair, rolled):
        rolled_1 = pltpu.roll(rolled, 1, 1)
        rolled_2 = pltpu.roll(rolled_1, 1, 1)
        at = pl.ds(pl.multiple_of(pair * 16, 16), 16)
        code_ref[0, at, :] = jnp.concatenate([rolled, rolled_1], 0).astype(jnp.bfloat16)
        code_ref[1, at, :] = jnp.concatenate([rolled_1, rolled_2], 0).astype(jnp.bfloat16)
        return rolled_2

    lax.fori_loop(0, CODE_ROWS // 16, fill, base_ref[...])


def kernel(
    periods, peers, record, base, lags, head, rest, out,
    code, seg, sel, even, odd, own, half_out, half_in, ready, got, late,
    main_sem, extra_sem, half_send, half_recv, send_sem, recv_sem, late_send, late_recv,
):
    me = lax.axis_index("tm")
    hyd = lax.axis_index("hyd")
    delays = DELAYS // peers
    beams = BEAMS // 2
    width = record.shape[1]

    barrier = pltpu.get_barrier_semaphore()
    for step in range(1, peers):
        pl.semaphore_signal(
            barrier, inc=1, device_id={"tm": lax.rem(me + step, peers)}, device_id_type=MESH
        )
    pl.semaphore_signal(barrier, inc=1, device_id={"hyd": 1 - hyd}, device_id_type=MESH)

    def main_copy(period, slot):
        start = pl.multiple_of((period * CODE) // 16 * 16, 16)
        return pltpu.make_async_copy(
            record.at[pl.ds(start, MAIN)], seg.at[slot, pl.ds(0, MAIN)], main_sem.at[slot]
        )

    def extra_copy(period, slot):
        start = pl.multiple_of((period * CODE) // 16 * 16 + MAIN, 16)
        return pltpu.make_async_copy(
            record.at[pl.ds(start, EXTRA)], seg.at[slot, pl.ds(MAIN, EXTRA)], extra_sem.at[slot]
        )

    def late_copy():
        return pltpu.make_async_remote_copy(
            src_ref=head, dst_ref=late, send_sem=late_send, recv_sem=late_recv,
            device_id={"tm": lax.max(me - 1, 0)}, device_id_type=MESH,
        )

    def half_copy(period):
        return pltpu.make_async_remote_copy(
            src_ref=half_out.at[period], dst_ref=half_in.at[period],
            send_sem=half_send.at[period], recv_sem=half_recv.at[period],
            device_id={"hyd": 1 - hyd}, device_id_type=MESH,
        )

    def out_copy(period, peer):
        return pltpu.make_async_remote_copy(
            src_ref=ready.at[period, pl.ds(pl.multiple_of(peer * delays, 16), delays)],
            dst_ref=got.at[me * periods + period],
            send_sem=send_sem.at[peer, period], recv_sem=recv_sem.at[me, period],
            device_id={"tm": peer}, device_id_type=MESH,
        )

    def in_wait(period, peer):
        pltpu.make_async_remote_copy(
            src_ref=ready.at[period, pl.ds(0, delays)],
            dst_ref=got.at[peer * periods + period],
            send_sem=send_sem.at[peer, period], recv_sem=recv_sem.at[peer, period],
            device_id={"tm": peer}, device_id_type=MESH,
        ).wait_recv()

    main_copy(0, 0).start()
    extra_copy(0, 0).start()
    build_code(base, code)
    for offset in range(MAXLAG):
        sel[pl.ds(offset * width, width), :] = jnp.where(
            lags[...] == offset, 1.0, 0.0
        ).astype(jnp.bfloat16)

    pl.semaphore_wait(barrier, peers)

    @pl.when(me > 0)
    def _():
        late_copy().start()

    def pass_on(period):
        half_copy(period).wait_recv()
        total = own[...] + half_in[period].astype(jnp.float32)
        own[...] = total
        for j in range(ROWS):
            ready[period, pl.ds(j * STEP, STEP), :] = own[
                pl.ds(j, STEP, stride=ROWS), :
            ].astype(jnp.bfloat16)
        got[me * periods + period] = ready[
            period, pl.ds(pl.multiple_of(me * delays, 16), delays), :
        ]

        def send(step, carry):
            out_copy(period, lax.rem(me + step, peers)).start()
            return carry

        lax.fori_loop(1, peers, send, 0)

    def one_period(period, carry):
        slot = lax.rem(period, 2)
        main_copy(period, slot).wait()

        @pl.when(period < periods - 1)
        def _():
            extra_copy(period, slot).wait()
            main_copy(period + 1, 1 - slot).start()

        @pl.when(period < periods - 2)
        def _():
            extra_copy(period + 1, 1 - slot).start()

        @pl.when(period == periods - 1)
        def _():
            @pl.when(me < peers - 1)
            def _():
                late_copy().wait_recv()

            @pl.when(me == peers - 1)
            def _():
                late[...] = jnp.zeros_like(late)

            seg[slot, pl.ds(MAIN + 16, LATE - 16), :] = late[pl.ds(16, LATE - 16), :]
            seg[slot, pl.ds(MAIN, 16), :] = late[pl.ds(0, 16), :] + rest[...]
            seg[slot, pl.ds(MAIN + LATE, EXTRA - LATE), :] = jnp.zeros(
                (EXTRA - LATE, width), jnp.bfloat16
            )

        lead = lax.rem(period * CODE, 16)
        parity = lax.rem(lead, 2)
        first = pl.multiple_of((lead - parity) * ROWS, 16)
        profile = jnp.dot(
            code[parity, pl.ds(first, OUT_ROWS), :], seg[slot], preferred_element_type=jnp.float32
        ) * (1.0 / math.sqrt(CODE))
        row = lax.broadcasted_iota(jnp.int32, (ROWS * MAXLAG, width), 0)
        edge = jnp.where(row % ROWS == ROWS - 1, 0.0, profile[DELAYS:])
        profile = jnp.concatenate([profile[:DELAYS], edge], 0)
        even[...] = profile.astype(jnp.bfloat16)
        odd[...] = profile[ROWS : OUT_ROWS - ROWS].astype(jnp.bfloat16)
        shifted = []
        for offset in range(MAXLAG):
            source = odd if offset % 2 else even
            shifted.append(source[pl.ds(offset // 2 * 16, DELAYS), :])
        beam = jnp.dot(
            jnp.concatenate(shifted, 1), sel[...], preferred_element_type=jnp.float32
        ) * (1.0 / math.sqrt(HYDRO))

        @pl.when(period > 0)
        def _():
            pass_on(period - 1)

        first_half, second_half = beam[:, :beams], beam[:, beams:]
        own[...] = jnp.where(hyd == 0, first_half, second_half)
        half_out[period] = jnp.where(hyd == 0, second_half, first_half).astype(jnp.bfloat16)
        half_copy(period).start()
        return carry

    lax.fori_loop(0, periods, one_period, 0)
    pass_on(periods - 1)

    @pl.when(me > 0)
    def _():
        late_copy().wait_send()

    def finish(period, carry):
        half_copy(period).wait_send()

        def one(step, carry):
            peer = lax.rem(me + step, peers)
            in_wait(period, peer)
            out_copy(period, peer).wait_send()
            return carry

        return lax.fori_loop(1, peers, one, carry)

    lax.fori_loop(0, periods, finish, 0)
    out[...] = got[...]


def beam_sums(record, chips, steer_lags, peers):
    rows, width = record.shape
    periods = rows // CODE
    delays = DELAYS // peers
    beams = BEAMS // 2
    whole_rows = rows // 16 * 16
    over = rows - whole_rows
    code = chips.astype(jnp.float32)
    base = jnp.stack(
        [jnp.pad(code, (STEP * j, WIDTH - CODE - STEP * j)) for j in range(ROWS)]
    )
    head = jnp.pad(record[: DELAYS - 1], ((over, LATE - over - DELAYS + 1), (0, 0)))
    rest = jnp.pad(record[whole_rows:], ((0, 16 - over), (0, 0)))
    vmem = pl.BlockSpec(memory_space=pltpu.VMEM)
    dma = pltpu.SemaphoreType.DMA
    bf16, f32 = jnp.bfloat16, jnp.float32
    flops = 2 * periods * (OUT_ROWS * WIDTH * width + DELAYS * MAXLAG * width * BEAMS)
    return pl.pallas_call(
        functools.partial(kernel, periods, peers),
        out_shape=jax.ShapeDtypeStruct((PERIODS, delays, beams), bf16),
        in_specs=[pl.BlockSpec(memory_space=pl.ANY), vmem, vmem, vmem, vmem],
        out_specs=vmem,
        scratch_shapes=[
            pltpu.VMEM((2, CODE_ROWS, WIDTH), bf16),
            pltpu.VMEM((2, WIDTH, width), bf16),
            pltpu.VMEM((MAXLAG * width, BEAMS), bf16),
            pltpu.VMEM((OUT_ROWS, width), bf16),
            pltpu.VMEM((OUT_ROWS - 2 * ROWS, width), bf16),
            pltpu.VMEM((DELAYS, beams), f32),
            pltpu.VMEM((periods, DELAYS, beams), bf16),
            pltpu.VMEM((periods, DELAYS, beams), bf16),
            pltpu.VMEM((periods, DELAYS, beams), bf16),
            pltpu.VMEM((PERIODS, delays, beams), bf16),
            pltpu.VMEM((LATE, width), bf16),
            dma((2,)), dma((2,)), dma((periods,)), dma((periods,)),
            dma((peers, periods)), dma((peers, periods)), dma, dma,
        ],
        compiler_params=pltpu.CompilerParams(
            collective_id=0, has_side_effects=True, vmem_limit_bytes=60 * 1024 * 1024
        ),
        cost_estimate=pl.CostEstimate(
            flops=flops, bytes_accessed=2 * rows * width, transcendentals=0
        ),
    )(record, base, steer_lags, head, rest)


def power_kernel(delays, table, got, out, wide):
    wide[...] = got[...].astype(jnp.float32)
    group = 4
    for first in range(0, delays, group):
        columns = [
            wide[pl.ds(first + k, PERIODS, stride=delays), :].astype(jnp.bfloat16)
            for k in range(group)
        ]
        spectrum = jnp.dot(
            table[...], jnp.concatenate(columns, 1), preferred_element_type=jnp.float32
        )
        real, imag = spectrum[:PERIODS], spectrum[PERIODS:]
        power = real * real + imag * imag
        beams = power.shape[1] // group
        for k in range(group):
            out[pl.ds(first + k, PERIODS, stride=delays), :] = power[
                :, k * beams : (k + 1) * beams
            ]


def dft_table(length):
    freq = jnp.arange(length, dtype=jnp.int32)
    phase = (freq[:, None] * freq[None, :] % length).astype(jnp.float32) * (2.0 * math.pi / length)
    weight = 1.0 / math.sqrt(length)
    return jnp.concatenate([jnp.cos(phase) * weight, -jnp.sin(phase) * weight], 0).astype(
        jnp.bfloat16
    )


def body(record, chips, steer_lags):
    got = beam_sums(record, chips, steer_lags, lax.axis_size("tm"))
    periods, delays, beams = got.shape
    vmem = pl.BlockSpec(memory_space=pltpu.VMEM)
    power = pl.pallas_call(
        functools.partial(power_kernel, delays),
        out_shape=jax.ShapeDtypeStruct((periods * delays, beams), jnp.float32),
        in_specs=[vmem, vmem],
        out_specs=vmem,
        scratch_shapes=[pltpu.VMEM((periods * delays, beams), jnp.float32)],
        compiler_params=pltpu.CompilerParams(vmem_limit_bytes=32 * 1024 * 1024),
    )(dft_table(PERIODS), got.reshape(periods * delays, beams))
    return power.reshape(periods, delays, beams)


def solution(mesh):
    in_specs = (P(("runs", "tm"), "hyd"), P(), P("hyd", None))
    out_specs = P("runs", "tm", "hyd")
    return jax.shard_map(body, mesh=mesh, in_specs=in_specs, out_specs=out_specs, check_vma=False)
```

```python
import functools
import math

import jax
import jax.numpy as jnp
from jax import lax
from jax.experimental import pallas as pl
from jax.experimental.pallas import tpu as pltpu
from jax.sharding import PartitionSpec as P

CODE = 4095
HYDRO = 1024
DELAYS = 512
PERIODS = 64
BEAMS = 256
MAXLAG = 8

ROWS = 8
STEP = DELAYS // ROWS
OUT_ROWS = ROWS * (STEP + MAXLAG)
PAIR_ROWS = DELAYS + 2 * ROWS
CODE_ROWS = OUT_ROWS + ROWS * 14
WIDTH = 4736
MAIN = 4096
EXTRA = WIDTH - MAIN
LATE = 528
MESH = pl.DeviceIdType.MESH


def build_code(chips_ref, code_ref):
    def fill(pair, rolled):
        rolled_1 = pltpu.roll(rolled, 1, 1)
        rolled_2 = pltpu.roll(rolled_1, 1, 1)
        at = pl.ds(pl.multiple_of(pair * 16, 16), 16)
        code_ref[0, at, :] = jnp.concatenate([rolled, rolled_1], 0).astype(jnp.bfloat16)
        code_ref[1, at, :] = jnp.concatenate([rolled_1, rolled_2], 0).astype(jnp.bfloat16)
        return rolled_2

    chips = jnp.broadcast_to(chips_ref[...], (ROWS, WIDTH))
    row = lax.broadcasted_iota(jnp.int32, (ROWS, WIDTH), 0)
    base = chips
    for j in range(1, ROWS):
        base = jnp.where(row == j, pltpu.roll(chips, STEP * j, 1), base)
    lax.fori_loop(0, CODE_ROWS // 16, fill, base)


def kernel(
    periods, peers, record, chip_row, lags, rest, out,
    code, seg, sel, even, own, half_out, half_in, ready, got, late,
    main_sem, extra_sem, half_send, half_recv, send_sem, recv_sem, late_send, late_recv,
):
    me = lax.axis_index("tm")
    hyd = lax.axis_index("hyd")
    delays = DELAYS // peers
    beams = BEAMS // 2
    width = record.shape[1]

    barrier = pltpu.get_barrier_semaphore()
    for step in range(1, peers):
        pl.semaphore_signal(
            barrier, inc=1, device_id={"tm": lax.rem(me + step, peers)}, device_id_type=MESH
        )
    pl.semaphore_signal(barrier, inc=1, device_id={"hyd": 1 - hyd}, device_id_type=MESH)

    def main_copy(period, slot):
        start = pl.multiple_of((period * CODE) // 16 * 16, 16)
        return pltpu.make_async_copy(
            record.at[pl.ds(start, MAIN)], seg.at[slot, pl.ds(0, MAIN)], main_sem.at[slot]
        )

    def extra_copy(period, slot):
        start = pl.multiple_of((period * CODE) // 16 * 16 + MAIN, 16)
        return pltpu.make_async_copy(
            record.at[pl.ds(start, EXTRA)], seg.at[slot, pl.ds(MAIN, EXTRA)], extra_sem.at[slot]
        )

    def late_copy():
        return pltpu.make_async_remote_copy(
            src_ref=record.at[pl.ds(0, DELAYS)], dst_ref=late, send_sem=late_send, recv_sem=late_recv,
            device_id={"tm": lax.max(me - 1, 0)}, device_id_type=MESH,
        )

    def half_copy(period):
        return pltpu.make_async_remote_copy(
            src_ref=half_out.at[period], dst_ref=half_in.at[period],
            send_sem=half_send.at[period], recv_sem=half_recv.at[period],
            device_id={"hyd": 1 - hyd}, device_id_type=MESH,
        )

    def out_copy(period, peer):
        return pltpu.make_async_remote_copy(
            src_ref=ready.at[period, pl.ds(pl.multiple_of(peer * delays, 16), delays)],
            dst_ref=got.at[me * periods + period],
            send_sem=send_sem.at[peer, period], recv_sem=recv_sem.at[me, period],
            device_id={"tm": peer}, device_id_type=MESH,
        )

    def in_wait(period, peer):
        pltpu.make_async_remote_copy(
            src_ref=ready.at[period, pl.ds(0, delays)],
            dst_ref=got.at[peer * periods + period],
            send_sem=send_sem.at[peer, period], recv_sem=recv_sem.at[peer, period],
            device_id={"tm": peer}, device_id_type=MESH,
        ).wait_recv()

    main_copy(0, 0).start()
    extra_copy(0, 0).start()
    build_code(chip_row, code)
    for offset in range(MAXLAG):
        sel[pl.ds(offset // 2 * width, width), pl.ds(offset % 2 * BEAMS, BEAMS)] = jnp.where(
            lags[...] == offset, 1.0, 0.0
        ).astype(jnp.bfloat16)

    pl.semaphore_wait(barrier, peers)

    @pl.when(me > 0)
    def _():
        late_copy().start()

    def pass_on(period):
        half_copy(period).wait_recv()
        total = own[...] + half_in[period].astype(jnp.float32)
        own[...] = total
        for j in range(ROWS):
            ready[period, pl.ds(j * STEP, STEP), :] = own[
                pl.ds(j, STEP, stride=ROWS), :
            ].astype(jnp.bfloat16)
        got[me * periods + period] = ready[
            period, pl.ds(pl.multiple_of(me * delays, 16), delays), :
        ]

        def send(step, carry):
            out_copy(period, lax.rem(me + step, peers)).start()
            return carry

        lax.fori_loop(1, peers, send, 0)

    def one_period(period, carry):
        slot = lax.rem(period, 2)
        main_copy(period, slot).wait()

        @pl.when(period < periods - 1)
        def _():
            extra_copy(period, slot).wait()
            main_copy(period + 1, 1 - slot).start()

        @pl.when(period < periods - 2)
        def _():
            extra_copy(period + 1, 1 - slot).start()

        @pl.when(period == periods - 1)
        def _():
            @pl.when(me < peers - 1)
            def _():
                late_copy().wait_recv()

            @pl.when(me == peers - 1)
            def _():
                late[...] = jnp.zeros_like(late)

            over = record.shape[0] % 16
            seg[slot, pl.ds(MAIN, LATE), :] = jnp.concatenate(
                [
                    rest[...].astype(jnp.float32)[16 - over :],
                    late[...].astype(jnp.float32),
                    jnp.zeros((16 - over, width), jnp.float32),
                ],
                0,
            ).astype(jnp.bfloat16)
            seg[slot, pl.ds(MAIN + LATE, EXTRA - LATE), :] = jnp.zeros(
                (EXTRA - LATE, width), jnp.bfloat16
            )

        lead = lax.rem(period * CODE, 16)
        parity = lax.rem(lead, 2)
        first = pl.multiple_of((lead - parity) * ROWS, 16)
        profile = jnp.dot(
            code[parity, pl.ds(first, OUT_ROWS), :], seg[slot], preferred_element_type=jnp.float32
        ) * (1.0 / math.sqrt(CODE))
        row = lax.broadcasted_iota(jnp.int32, (ROWS * MAXLAG, width), 0)
        edge = jnp.where(row % ROWS == ROWS - 1, 0.0, profile[DELAYS:])
        profile = jnp.concatenate([profile[:DELAYS], edge], 0)
        even[...] = profile.astype(jnp.bfloat16)

        @pl.when(period > 0)
        def _():
            pass_on(period - 1)

        shifted = [even[pl.ds(pair * 16, PAIR_ROWS), :] for pair in range(MAXLAG // 2)]
        pairs = jnp.dot(
            jnp.concatenate(shifted, 1), sel[...], preferred_element_type=jnp.float32
        )
        beam = (pairs[:DELAYS, :BEAMS] + pairs[ROWS : ROWS + DELAYS, BEAMS:]) * (
            1.0 / math.sqrt(HYDRO)
        )
        first_half, second_half = beam[:, :beams], beam[:, beams:]
        own[...] = jnp.where(hyd == 0, first_half, second_half)
        half_out[period] = jnp.where(hyd == 0, second_half, first_half).astype(jnp.bfloat16)
        half_copy(period).start()
        return carry

    lax.fori_loop(0, periods, one_period, 0)
    pass_on(periods - 1)

    @pl.when(me > 0)
    def _():
        late_copy().wait_send()

    def finish(period, carry):
        half_copy(period).wait_send()

        def one(step, carry):
            peer = lax.rem(me + step, peers)
            in_wait(period, peer)
            out_copy(period, peer).wait_send()
            return carry

        return lax.fori_loop(1, peers, one, carry)

    lax.fori_loop(0, periods, finish, 0)
    out[...] = got[...]


def beam_sums(record, chips, steer_lags, peers):
    rows, width = record.shape
    periods = rows // CODE
    delays = DELAYS // peers
    beams = BEAMS // 2
    chip_row = jnp.pad(chips.astype(jnp.float32), (0, WIDTH - CODE))[None]
    rest = record[rows - 16 :]
    vmem = pl.BlockSpec(memory_space=pltpu.VMEM)
    dma = pltpu.SemaphoreType.DMA
    bf16, f32 = jnp.bfloat16, jnp.float32
    flops = 2 * periods * (OUT_ROWS * WIDTH * width + DELAYS * MAXLAG * width * BEAMS)
    return pl.pallas_call(
        functools.partial(kernel, periods, peers),
        out_shape=jax.ShapeDtypeStruct((PERIODS, delays, beams), bf16),
        in_specs=[pl.BlockSpec(memory_space=pl.ANY), vmem, vmem, vmem],
        out_specs=vmem,
        scratch_shapes=[
            pltpu.VMEM((2, CODE_ROWS, WIDTH), bf16),
            pltpu.VMEM((2, WIDTH, width), bf16),
            pltpu.VMEM((MAXLAG // 2 * width, 2 * BEAMS), bf16),
            pltpu.VMEM((OUT_ROWS, width), bf16),
            pltpu.VMEM((DELAYS, beams), f32),
            pltpu.VMEM((periods, DELAYS, beams), bf16),
            pltpu.VMEM((periods, DELAYS, beams), bf16),
            pltpu.VMEM((periods, DELAYS, beams), bf16),
            pltpu.VMEM((PERIODS, delays, beams), bf16),
            pltpu.VMEM((DELAYS, width), bf16),
            dma((2,)), dma((2,)), dma((periods,)), dma((periods,)),
            dma((peers, periods)), dma((peers, periods)), dma, dma,
        ],
        compiler_params=pltpu.CompilerParams(
            collective_id=0, has_side_effects=True, vmem_limit_bytes=60 * 1024 * 1024
        ),
        cost_estimate=pl.CostEstimate(
            flops=flops, bytes_accessed=2 * rows * width, transcendentals=0
        ),
    )(record, chip_row, steer_lags, rest)


def power_kernel(delays, table, got, out, wide):
    wide[...] = got[...].astype(jnp.float32)
    group = 4
    for first in range(0, delays, group):
        columns = [
            wide[pl.ds(first + k, PERIODS, stride=delays), :].astype(jnp.bfloat16)
            for k in range(group)
        ]
        spectrum = jnp.dot(
            table[...], jnp.concatenate(columns, 1), preferred_element_type=jnp.float32
        )
        real, imag = spectrum[:PERIODS], spectrum[PERIODS:]
        power = real * real + imag * imag
        beams = power.shape[1] // group
        for k in range(group):
            out[pl.ds(first + k, PERIODS, stride=delays), :] = power[
                :, k * beams : (k + 1) * beams
            ]


def dft_table(length):
    freq = jnp.arange(length, dtype=jnp.int32)
    phase = (freq[:, None] * freq[None, :] % length).astype(jnp.float32) * (2.0 * math.pi / length)
    weight = 1.0 / math.sqrt(length)
    return jnp.concatenate([jnp.cos(phase) * weight, -jnp.sin(phase) * weight], 0).astype(
        jnp.bfloat16
    )


def body(record, chips, steer_lags):
    got = beam_sums(record, chips, steer_lags, lax.axis_size("tm"))
    periods, delays, beams = got.shape
    vmem = pl.BlockSpec(memory_space=pltpu.VMEM)
    power = pl.pallas_call(
        functools.partial(power_kernel, delays),
        out_shape=jax.ShapeDtypeStruct((periods * delays, beams), jnp.float32),
        in_specs=[vmem, vmem],
        out_specs=vmem,
        scratch_shapes=[pltpu.VMEM((periods * delays, beams), jnp.float32)],
        compiler_params=pltpu.CompilerParams(vmem_limit_bytes=32 * 1024 * 1024),
    )(dft_table(PERIODS), got.reshape(periods * delays, beams))
    return power.reshape(periods, delays, beams)


def solution(mesh):
    in_specs = (P(("runs", "tm"), "hyd"), P(), P("hyd", None))
    out_specs = P("runs", "tm", "hyd")
    return jax.shard_map(body, mesh=mesh, in_specs=in_specs, out_specs=out_specs, check_vma=False)
```

```python
import functools
import math

import jax
import jax.numpy as jnp
from jax import lax
from jax.experimental import pallas as pl
from jax.experimental.pallas import tpu as pltpu
from jax.sharding import PartitionSpec as P

CODE = 4095
HYDRO = 1024
DELAYS = 512
PERIODS = 64
BEAMS = 256
MAXLAG = 8

ROWS = 8
STEP = DELAYS // ROWS
OUT_ROWS = ROWS * (STEP + MAXLAG)
PAIR_ROWS = DELAYS + 2 * ROWS
CODE_ROWS = OUT_ROWS + ROWS * 14
WIDTH = 4736
MAIN = 4096
EXTRA = WIDTH - MAIN
LATE = 528
MESH = pl.DeviceIdType.MESH


def build_code(chips_ref, code_ref):
    def fill(pair, rolled):
        rolled_1 = pltpu.roll(rolled, 1, 1)
        rolled_2 = pltpu.roll(rolled, 2, 1)
        at = pl.ds(pl.multiple_of(pair * 16, 16), 16)
        code_ref[0, at, :] = jnp.concatenate([rolled, rolled_1], 0).astype(jnp.bfloat16)
        code_ref[1, at, :] = jnp.concatenate([rolled_1, rolled_2], 0).astype(jnp.bfloat16)
        return rolled_2

    chips = jnp.broadcast_to(chips_ref[...], (ROWS, WIDTH))
    row = lax.broadcasted_iota(jnp.int32, (ROWS, WIDTH), 0)
    base = chips
    for j in range(1, ROWS):
        base = jnp.where(row == j, pltpu.roll(chips, STEP * j, 1), base)
    lax.fori_loop(0, CODE_ROWS // 16, fill, base)


def kernel(
    periods, peers, record, chip_row, lags, rest, out,
    code, seg, sel, even, own, half_out, half_in, ready, got, late,
    main_sem, extra_sem, half_send, half_recv, send_sem, recv_sem, late_send, late_recv,
):
    me = lax.axis_index("tm")
    hyd = lax.axis_index("hyd")
    delays = DELAYS // peers
    beams = BEAMS // 2
    width = record.shape[1]

    barrier = pltpu.get_barrier_semaphore()
    for step in range(1, peers):
        pl.semaphore_signal(
            barrier, inc=1, device_id={"tm": lax.rem(me + step, peers)}, device_id_type=MESH
        )
    pl.semaphore_signal(barrier, inc=1, device_id={"hyd": 1 - hyd}, device_id_type=MESH)

    def main_copy(period, slot):
        start = pl.multiple_of((period * CODE) // 16 * 16, 16)
        return pltpu.make_async_copy(
            record.at[pl.ds(start, MAIN)], seg.at[slot, pl.ds(0, MAIN)], main_sem.at[slot]
        )

    def extra_copy(period, slot):
        start = pl.multiple_of((period * CODE) // 16 * 16 + MAIN, 16)
        return pltpu.make_async_copy(
            record.at[pl.ds(start, EXTRA)], seg.at[slot, pl.ds(MAIN, EXTRA)], extra_sem.at[slot]
        )

    def late_copy():
        return pltpu.make_async_remote_copy(
            src_ref=record.at[pl.ds(0, DELAYS)], dst_ref=late, send_sem=late_send, recv_sem=late_recv,
            device_id={"tm": lax.max(me - 1, 0)}, device_id_type=MESH,
        )

    def half_copy(period):
        return pltpu.make_async_remote_copy(
            src_ref=half_out.at[period], dst_ref=half_in.at[period],
            send_sem=half_send.at[period], recv_sem=half_recv.at[period],
            device_id={"hyd": 1 - hyd}, device_id_type=MESH,
        )

    def out_copy(period, peer):
        return pltpu.make_async_remote_copy(
            src_ref=ready.at[period, pl.ds(pl.multiple_of(peer * delays, 16), delays)],
            dst_ref=got.at[me * periods + period],
            send_sem=send_sem.at[peer, period], recv_sem=recv_sem.at[me, period],
            device_id={"tm": peer}, device_id_type=MESH,
        )

    def in_wait(period, peer):
        pltpu.make_async_remote_copy(
            src_ref=ready.at[period, pl.ds(0, delays)],
            dst_ref=got.at[peer * periods + period],
            send_sem=send_sem.at[peer, period], recv_sem=recv_sem.at[peer, period],
            device_id={"tm": peer}, device_id_type=MESH,
        ).wait_recv()

    main_copy(0, 0).start()
    extra_copy(0, 0).start()
    build_code(chip_row, code)
    for offset in range(MAXLAG):
        sel[pl.ds(offset // 2 * width, width), pl.ds(offset % 2 * BEAMS, BEAMS)] = jnp.where(
            lags[...] == offset, 1.0, 0.0
        ).astype(jnp.bfloat16)

    pl.semaphore_wait(barrier, peers)

    @pl.when(me > 0)
    def _():
        late_copy().start()

    def pass_on(period):
        half_copy(period).wait_recv()
        total = own[...] + half_in[period].astype(jnp.float32)
        own[...] = total
        for j in range(ROWS):
            ready[period, pl.ds(j * STEP, STEP), :] = own[
                pl.ds(j, STEP, stride=ROWS), :
            ].astype(jnp.bfloat16)
        got[me * periods + period] = ready[
            period, pl.ds(pl.multiple_of(me * delays, 16), delays), :
        ]

        def send(step, carry):
            out_copy(period, lax.rem(me + step, peers)).start()
            return carry

        lax.fori_loop(1, peers, send, 0)

    def one_period(period, carry):
        slot = lax.rem(period, 2)
        main_copy(period, slot).wait()

        @pl.when(period < periods - 1)
        def _():
            extra_copy(period, slot).wait()
            main_copy(period + 1, 1 - slot).start()

        @pl.when(period < periods - 2)
        def _():
            extra_copy(period + 1, 1 - slot).start()

        @pl.when(period == periods - 1)
        def _():
            @pl.when(me < peers - 1)
            def _():
                late_copy().wait_recv()

            @pl.when(me == peers - 1)
            def _():
                late[...] = jnp.zeros_like(late)

            over = record.shape[0] % 16
            seg[slot, pl.ds(MAIN, LATE), :] = jnp.concatenate(
                [
                    rest[...].astype(jnp.float32)[16 - over :],
                    late[...].astype(jnp.float32),
                    jnp.zeros((16 - over, width), jnp.float32),
                ],
                0,
            ).astype(jnp.bfloat16)
            seg[slot, pl.ds(MAIN + LATE, EXTRA - LATE), :] = jnp.zeros(
                (EXTRA - LATE, width), jnp.bfloat16
            )

        lead = lax.rem(period * CODE, 16)
        parity = lax.rem(lead, 2)
        first = pl.multiple_of((lead - parity) * ROWS, 16)
        profile = jnp.dot(
            code[parity, pl.ds(first, OUT_ROWS), :], seg[slot], preferred_element_type=jnp.float32
        ) * (1.0 / math.sqrt(CODE))
        row = lax.broadcasted_iota(jnp.int32, (ROWS * MAXLAG, width), 0)
        edge = jnp.where(row % ROWS == ROWS - 1, 0.0, profile[DELAYS:])
        profile = jnp.concatenate([profile[:DELAYS], edge], 0)
        even[...] = profile.astype(jnp.bfloat16)

        @pl.when(period > 0)
        def _():
            pass_on(period - 1)

        shifted = [even[pl.ds(pair * 16, PAIR_ROWS), :] for pair in range(MAXLAG // 2)]
        pairs = jnp.dot(
            jnp.concatenate(shifted, 1), sel[...], preferred_element_type=jnp.float32
        )
        beam = (pairs[:DELAYS, :BEAMS] + pairs[ROWS : ROWS + DELAYS, BEAMS:]) * (
            1.0 / math.sqrt(HYDRO)
        )
        first_half, second_half = beam[:, :beams], beam[:, beams:]
        own[...] = jnp.where(hyd == 0, first_half, second_half)
        half_out[period] = jnp.where(hyd == 0, second_half, first_half).astype(jnp.bfloat16)
        half_copy(period).start()
        return carry

    lax.fori_loop(0, periods, one_period, 0)
    pass_on(periods - 1)

    @pl.when(me > 0)
    def _():
        late_copy().wait_send()

    def finish(period, carry):
        half_copy(period).wait_send()

        def one(step, carry):
            peer = lax.rem(me + step, peers)
            in_wait(period, peer)
            out_copy(period, peer).wait_send()
            return carry

        return lax.fori_loop(1, peers, one, carry)

    lax.fori_loop(0, periods, finish, 0)
    out[...] = got[...]


def beam_sums(record, chips, steer_lags, peers):
    rows, width = record.shape
    periods = rows // CODE
    delays = DELAYS // peers
    beams = BEAMS // 2
    chip_row = jnp.pad(chips.astype(jnp.float32), (0, WIDTH - CODE))[None]
    rest = record[rows - 16 :]
    vmem = pl.BlockSpec(memory_space=pltpu.VMEM)
    dma = pltpu.SemaphoreType.DMA
    bf16, f32 = jnp.bfloat16, jnp.float32
    flops = 2 * periods * (OUT_ROWS * WIDTH * width + DELAYS * MAXLAG * width * BEAMS)
    return pl.pallas_call(
        functools.partial(kernel, periods, peers),
        out_shape=jax.ShapeDtypeStruct((PERIODS, delays, beams), bf16),
        in_specs=[pl.BlockSpec(memory_space=pl.ANY), vmem, vmem, vmem],
        out_specs=vmem,
        scratch_shapes=[
            pltpu.VMEM((2, CODE_ROWS, WIDTH), bf16),
            pltpu.VMEM((2, WIDTH, width), bf16),
            pltpu.VMEM((MAXLAG // 2 * width, 2 * BEAMS), bf16),
            pltpu.VMEM((OUT_ROWS, width), bf16),
            pltpu.VMEM((DELAYS, beams), f32),
            pltpu.VMEM((periods, DELAYS, beams), bf16),
            pltpu.VMEM((periods, DELAYS, beams), bf16),
            pltpu.VMEM((periods, DELAYS, beams), bf16),
            pltpu.VMEM((PERIODS, delays, beams), bf16),
            pltpu.VMEM((DELAYS, width), bf16),
            dma((2,)), dma((2,)), dma((periods,)), dma((periods,)),
            dma((peers, periods)), dma((peers, periods)), dma, dma,
        ],
        compiler_params=pltpu.CompilerParams(
            collective_id=0, has_side_effects=True, vmem_limit_bytes=60 * 1024 * 1024
        ),
        cost_estimate=pl.CostEstimate(
            flops=flops, bytes_accessed=2 * rows * width, transcendentals=0
        ),
    )(record, chip_row, steer_lags, rest)


def power_kernel(delays, table, got, out, wide):
    wide[...] = got[...].astype(jnp.float32)
    group = 4
    for first in range(0, delays, group):
        columns = [
            wide[pl.ds(first + k, PERIODS, stride=delays), :].astype(jnp.bfloat16)
            for k in range(group)
        ]
        spectrum = jnp.dot(
            table[...], jnp.concatenate(columns, 1), preferred_element_type=jnp.float32
        )
        real, imag = spectrum[:PERIODS], spectrum[PERIODS:]
        power = real * real + imag * imag
        beams = power.shape[1] // group
        for k in range(group):
            out[pl.ds(first + k, PERIODS, stride=delays), :] = power[
                :, k * beams : (k + 1) * beams
            ]


def dft_table(length):
    freq = jnp.arange(length, dtype=jnp.int32)
    phase = (freq[:, None] * freq[None, :] % length).astype(jnp.float32) * (2.0 * math.pi / length)
    weight = 1.0 / math.sqrt(length)
    return jnp.concatenate([jnp.cos(phase) * weight, -jnp.sin(phase) * weight], 0).astype(
        jnp.bfloat16
    )


def body(record, chips, steer_lags):
    got = beam_sums(record, chips, steer_lags, lax.axis_size("tm"))
    periods, delays, beams = got.shape
    vmem = pl.BlockSpec(memory_space=pltpu.VMEM)
    power = pl.pallas_call(
        functools.partial(power_kernel, delays),
        out_shape=jax.ShapeDtypeStruct((periods * delays, beams), jnp.float32),
        in_specs=[vmem, vmem],
        out_specs=vmem,
        scratch_shapes=[pltpu.VMEM((periods * delays, beams), jnp.float32)],
        compiler_params=pltpu.CompilerParams(vmem_limit_bytes=32 * 1024 * 1024),
    )(dft_table(PERIODS), got.reshape(periods * delays, beams))
    return power.reshape(periods, delays, beams)


def solution(mesh):
    in_specs = (P(("runs", "tm"), "hyd"), P(), P("hyd", None))
    out_specs = P("runs", "tm", "hyd")
    return jax.shard_map(body, mesh=mesh, in_specs=in_specs, out_specs=out_specs, check_vma=False)
```
